32 devices in a mesh: seq: 8 (over z, x), head: 4 (over y, core).
Axes of the slice: x: 2, y: 2, z: 4, core: 2. Of those that a mesh axis runs over, the one named last changes fastest.
Arguments:
- inputs: bfloat16 [8192, 8192], P('seq', 'head'), may hold values from -6 to 6
- in_map: bfloat16 [8192, 128], P('seq'), may hold values from -1.25 to 1.25
- out_map: bfloat16 [8192, 128], P('seq'), may hold values from -1.25 to 1.25
- log_decay: float32 [64, 8192], P('head', 'seq'), may hold values from -0.8 to 0, as said below
- cotangent: bfloat16 [8192, 8192], P('seq', 'head'), may hold values from -0.4375 to 0.4375
Outputs:
- grad_inputs: float32 [8192, 8192], P('seq', 'head')
- grad_in_map: float32 [8192, 128], P(('seq', 'head'))
- grad_out_map: float32 [8192, 128], P(('seq', 'head'))
- grad_decay: float32 [64, 8192], P('head', 'seq')
The draws below stay inside these ranges and needn't reach their ends.
Inputs may be any that keep to these rules, and one draw needn't show every extreme that they name: `log_decay`: entries are negative.
All inputs are finite; a program needn't handle non-finite values.
Results may differ from the reference program's by a relative error of at most 0.00035.
Values sent between devices are 32-bit elements; how exact they have to be, the bound alone decides.
A program may use at most 128 MiB of HBM per device.

```python
import math
import jax
import jax.numpy as jnp
from jax import lax

HEADS = 64
HEAD_DIM = 128
STATE = 128
BLOCK = 512
TOK_DEV = 1024
TOKEN_COUNT = 8192


def draw_log_decay(key, part):
    split_random_keys = jax.random.split(key, 7)
    slow_flag = jax.random.randint(split_random_keys[0], (HEADS, 1), 0, 2).astype(jnp.float32)
    slow_rate = jax.random.uniform(split_random_keys[1], (HEADS, 1), jnp.float32, 0.05, 0.3) * (math.log(10.0) / TOKEN_COUNT)
    fast_rate = jax.random.uniform(split_random_keys[2], (HEADS, 1), jnp.float32, 1.0 / 50.0, 1.0 / 30.0)
    baseline_rate = slow_flag * slow_rate + (1.0 - slow_flag) * fast_rate
    jaggedness = jnp.exp(jax.random.uniform(split_random_keys[3], (HEADS, TOKEN_COUNT), jnp.float32, -0.69, 0.69))
    shard_count = TOKEN_COUNT // TOK_DEV
    per_device_factor = jnp.repeat(jax.random.uniform(split_random_keys[4], (1, shard_count), jnp.float32, 0.5, 1.5), TOK_DEV, axis=1)
    spike_positions = jax.random.randint(split_random_keys[5], (2,), 0, TOKEN_COUNT)
    spike_depth = jax.random.uniform(split_random_keys[6], (2,), jnp.float32, 0.22, 0.69)
    locations = jnp.arange(TOKEN_COUNT)
    spike_events = jnp.sum(jnp.where(locations[None, :] == spike_positions[:, None], spike_depth[:, None], 0.0), axis=0)
    return -(baseline_rate * jaggedness * per_device_factor) - spike_events[None, :]


def shard_levels(own_key, extent, cuts, low, high):
    factor_of = 1.0
    for dim, blocks in cuts:
        draws = jax.random.uniform(jax.random.fold_in(jax.random.fold_in(own_key, 6), dim), (blocks,), jnp.float32, low / len(cuts), high / len(cuts))
        factor_of = factor_of * jnp.repeat(jnp.exp(draws), extent[dim] // blocks).reshape((-1,) + (1,) * (len(extent) - 1 - dim))
    return factor_of


def noise(stream_key, dims, width, limit, shards=(), held_as=jnp.bfloat16):
    result = width * jax.random.normal(stream_key, dims, jnp.float32)
    if shards:
        result = result * shard_levels(stream_key, dims, shards, -0.22, 0.18)
    return jnp.clip(result, -limit, limit).astype(held_as)


def setup_inputs(seed: int = 0) -> dict:
    streams_of = jax.random.split(jax.random.key(seed), 6)
    inputs = noise(streams_of[0], (TOKEN_COUNT, HEADS * HEAD_DIM), 1.0, 6.0, ((0, 8), (1, 4)))
    in_map = noise(streams_of[1], (TOKEN_COUNT, STATE), (STATE ** -0.5), 1.25, ((0, 8),))
    out_map = noise(streams_of[2], (TOKEN_COUNT, STATE), (STATE ** -0.5), 1.25, ((0, 8),))
    log_decay = draw_log_decay(jax.random.fold_in(streams_of[5], 71), 0)
    cotangent = noise(streams_of[4], (TOKEN_COUNT, HEADS * HEAD_DIM), 0.03, 0.4375, ((0, 8), (1, 4)))
    return dict(inputs=inputs, in_map=in_map, out_map=out_map, log_decay=log_decay, cotangent=cotangent)


highest = lax.Precision.HIGHEST

def block_forward(state, pieces):
    inputs_blk, in_blk, out_blk, rates = pieces
    stretch = rates.shape[1]
    locations = jnp.arange(stretch)
    causal = (locations[:, None] >= locations[None, :])[None]
    running = jnp.cumsum(rates, axis=1)
    gaps = running[:, :, None] - running[:, None, :]
    decays = jnp.where(causal, jnp.exp(jnp.where(causal, gaps, 0.0)), 0.0)
    scores = jnp.dot(out_blk, in_blk.T, precision=highest, preferred_element_type=jnp.float32)
    inside = jnp.einsum('hts,shp->thp', decays * scores[None], inputs_blk, precision=highest)
    outside = jnp.einsum('tn,hpn->thp', out_blk, state, precision=highest) * jnp.exp(running).T[:, :, None]
    to_end = jnp.exp(running[:, -1:] - running)
    new_state = jnp.exp(running[:, -1])[:, None, None] * state + jnp.einsum('shp,sn->hpn', inputs_blk * to_end.T[:, :, None], in_blk, precision=highest)
    return (new_state, inside + outside)

def forward(inputs, in_map, out_map, log_decay):
    stretch = min(BLOCK, 128)
    pieces_count = TOKEN_COUNT // stretch
    inputs_blocks = inputs.reshape(pieces_count, stretch, HEADS, HEAD_DIM)
    in_blocks = in_map.reshape(pieces_count, stretch, STATE)
    out_blocks = out_map.reshape(pieces_count, stretch, STATE)
    rate_blocks = log_decay.reshape(HEADS, pieces_count, stretch).transpose(1, 0, 2)
    initial = jnp.zeros((HEADS, HEAD_DIM, STATE), jnp.float32)
    final_state, outputs = lax.scan(jax.checkpoint(block_forward), initial, (inputs_blocks, in_blocks, out_blocks, rate_blocks))
    return outputs.reshape(TOKEN_COUNT, HEADS * HEAD_DIM)

def reference(inputs, in_map, out_map, log_decay, cotangent):
    outputs, pullback = jax.vjp(forward, inputs.astype(jnp.float32), in_map.astype(jnp.float32), out_map.astype(jnp.float32), log_decay)
    grads = pullback(cotangent.astype(jnp.float32))
    return (grads[0], grads[1], grads[2], grads[3])
```

```python
import functools

import jax
import jax.numpy as jnp
from jax import lax
from jax.experimental import pallas as pl
from jax.experimental.pallas import tpu as pltpu
from jax.sharding import PartitionSpec as P

MESH = pl.DeviceIdType.MESH
F32, BF16 = jnp.float32, jnp.bfloat16
HIGHEST = lax.Precision.HIGHEST
CHUNK = 128
GROUP = 4
SPLIT = 2
SKEW = 2
VMEM_BYTES = 56 * 1024 * 1024


def nn(a, b, **kw):
    return lax.dot_general(a, b, (((1,), (0,)), ((), ())), preferred_element_type=F32, **kw)


def nt(a, b, **kw):
    return lax.dot_general(a, b, (((1,), (1,)), ((), ())), preferred_element_type=F32, **kw)


def tn(a, b, **kw):
    return lax.dot_general(a, b, (((0,), (0,)), ((), ())), preferred_element_type=F32, **kw)


def split(v):
    hi = v.astype(BF16)
    return hi, (v - hi.astype(F32)).astype(BF16)


def order(strict=False):
    row = lax.broadcasted_iota(jnp.int32, (CHUNK, CHUNK), 0)
    col = lax.broadcasted_iota(jnp.int32, (CHUNK, CHUNK), 1)
    return row > col if strict else row >= col


def wide(v, width):
    rows, heads = v.shape
    return jnp.concatenate(
        [jnp.broadcast_to(v[:, h : h + 1], (rows, width)) for h in range(heads)], axis=1
    )


def decays(rates):
    run = nt(order().astype(F32), rates, precision=HIGHEST)
    mid = run[CHUNK // 2 - 1 : CHUNK // 2, :]
    f = jnp.exp(run - mid)
    return f, jnp.exp(mid - run), jnp.exp(mid), f[CHUNK - 1 : CHUNK, :]


def heads_of(v, width):
    return [v[:, h : h + width] for h in range(0, v.shape[1], width)]


def states_kernel(x_ref, b_ref, c_ref, rate_ref, dy_ref, s_ref, e_ref, total_ref):
    tokens, columns = x_ref.shape
    width = columns // rate_ref.shape[1]
    chunks = tokens // CHUNK
    state = adjoint = jnp.zeros((b_ref.shape[1], columns), F32)
    reach = jnp.ones((1, columns), F32)
    for j in range(chunks):
        rows = pl.ds(j * CHUNK, CHUNK)
        f, g, mid, last = decays(rate_ref[0, :, rows])
        mid, last = wide(mid, width), wide(last, width)
        b, c = b_ref[rows, :], c_ref[rows, :]
        gx_hi, gx_lo = split(wide(g, width) * x_ref[rows, :].astype(F32))
        fy_hi, fy_lo = split(wide(f, width) * dy_ref[rows, :].astype(F32))
        state = (last * mid) * state + last * (tn(b, gx_hi) + tn(b, gx_lo))
        adjoint = adjoint + (reach * mid) * (tn(c, fy_hi) + tn(c, fy_lo))
        reach = reach * (last * mid)
    for h, (s, e, r) in enumerate(
        zip(heads_of(state, width), heads_of(adjoint, width), heads_of(reach, width))
    ):
        s_ref[h] = s
        e_ref[h] = e
        total_ref[h] = jnp.broadcast_to(r, total_ref.shape[1:])


def chain_kernel(
    peers, s_ref, e_ref, total_ref, s_in, e_in, s_out, e_out, s_send, s_recv, e_send, e_recv
):
    me, lane = lax.axis_index("seq"), lax.axis_index("head")
    items = s_ref.shape[0]
    has_left, has_right = me > 0, me < peers - 1
    barrier = pltpu.get_barrier_semaphore()

    @pl.when(has_left)
    def _():
        pl.semaphore_signal(barrier, inc=1, device_id=(me - 1, lane), device_id_type=MESH)

    @pl.when(has_right)
    def _():
        pl.semaphore_signal(barrier, inc=1, device_id=(me + 1, lane), device_id_type=MESH)

    pl.semaphore_wait(barrier, jnp.where(has_left, 1, 0) + jnp.where(has_right, 1, 0))

    def forward(i):
        return pltpu.make_async_remote_copy(
            src_ref=s_out.at[i], dst_ref=s_in.at[i], send_sem=s_send.at[i], recv_sem=s_recv.at[i],
            device_id=(me + 1, lane), device_id_type=MESH,
        )

    def backward(i):
        return pltpu.make_async_remote_copy(
            src_ref=e_out.at[i], dst_ref=e_in.at[i], send_sem=e_send.at[i], recv_sem=e_recv.at[i],
            device_id=(me - 1, lane), device_id_type=MESH,
        )

    def pass_on(i, copy, has_source, has_target, local, come, out):
        @pl.when(has_source)
        def _():
            copy(i).wait_recv()

        @pl.when(jnp.logical_not(has_source))
        def _():
            come[i] = jnp.zeros(come.shape[1:], F32)

        @pl.when(has_target)
        def _():
            out[i] = total_ref[i // SPLIT][0:1, :] * come[i] + local[i]
            copy(i).start()

    def step(i, _):
        at_s, at_e = i - SKEW * me, i - SKEW * (peers - 1 - me)

        @pl.when(jnp.logical_and(at_s >= 0, at_s < items))
        def _():
            pass_on(at_s, forward, has_left, has_right, s_ref, s_in, s_out)

        @pl.when(jnp.logical_and(at_e >= 0, at_e < items))
        def _():
            pass_on(at_e, backward, has_right, has_left, e_ref, e_in, e_out)

        return 0

    lax.fori_loop(0, items + SKEW * (peers - 1), step, 0)

    def finish(i, _):
        @pl.when(has_right)
        def _():
            forward(i).wait_send()

        @pl.when(has_left)
        def _():
            backward(i).wait_send()

        return 0

    lax.fori_loop(0, items, finish, 0)


def grads_kernel(
    x_ref, b_ref, c_ref, rate_ref, dy_ref, s_ref, e_ref,
    gx_ref, gb_ref, gc_ref, rates_out, adjoints, fy_hi_ref, fy_lo_ref, joint,
):
    group = pl.program_id(0)
    tokens, columns = x_ref.shape
    heads = rate_ref.shape[1]
    width = columns // heads
    chunks = tokens // CHUNK
    causal = order()
    after = jnp.logical_not(order()).astype(F32)
    head_lane = lax.broadcasted_iota(jnp.int32, (CHUNK, heads), 1)

    @pl.when(group == 0)
    def _():
        gb_ref[...] = jnp.zeros_like(gb_ref)
        gc_ref[...] = jnp.zeros_like(gc_ref)
        joint[...] = jnp.zeros_like(joint)

    def per_head(v):
        out = jnp.zeros((CHUNK, heads), F32)
        for h, part in enumerate(heads_of(v, width)):
            out = jnp.where(head_lane == h, jnp.sum(part, axis=1, keepdims=True), out)
        return out

    adjoint = jnp.concatenate([e_ref[h] for h in range(heads)], axis=1)
    adjoints[chunks] = adjoint
    for j in reversed(range(chunks)):
        rows = pl.ds(j * CHUNK, CHUNK)
        f, g, mid, last = decays(rate_ref[0, :, rows])
        mid, last = wide(mid, width), wide(last, width)
        fy_hi, fy_lo = split(wide(f, width) * dy_ref[rows, :].astype(F32))
        fy_hi_ref[rows, :] = fy_hi
        fy_lo_ref[rows, :] = fy_lo
        c = c_ref[rows, :]
        adjoint = mid * (last * adjoint + (tn(c, fy_hi) + tn(c, fy_lo)))
        adjoints[j] = adjoint

    state = jnp.concatenate([s_ref[h] for h in range(heads)], axis=1)
    for j in range(chunks):
        rows = pl.ds(j * CHUNK, CHUNK)
        f, g, mid, last = decays(rate_ref[0, :, rows])
        mid, last = wide(mid, width), wide(last, width)
        g_wide = wide(g, width)
        b, c = b_ref[rows, :], c_ref[rows, :]
        gx = g_wide * x_ref[rows, :].astype(F32)
        gx_hi, gx_lo = split(gx)
        fy_hi, fy_lo = fy_hi_ref[rows, :], fy_lo_ref[rows, :]
        scores = jnp.where(causal, nt(c, b), 0.0)
        m_hi, m_lo = split(scores)
        t_hi, t_lo = split(scores.T)
        s_hi, s_lo = split(mid * state)
        e_hi, e_lo = split(last * adjoints[j + 1])
        y = nn(
            jnp.concatenate([m_hi, m_hi, m_lo, c, c], axis=1),
            jnp.concatenate([gx_hi, gx_lo, gx_hi, s_hi, s_lo], axis=0),
        )
        z = nn(
            jnp.concatenate([t_hi, t_hi, t_lo, b, b], axis=1),
            jnp.concatenate([fy_hi, fy_lo, fy_hi, e_hi, e_lo], axis=0),
        )
        gx_ref[rows, :] = g_wide * z
        fy = fy_hi.astype(F32) + fy_lo.astype(F32)
        turnover = per_head(gx * z - fy * y)
        crossing = per_head(adjoints[j] * state)
        rates_out[0, :, rows] = tn(turnover, after, precision=HIGHEST) + tn(
            crossing, jnp.ones((CHUNK, CHUNK), F32), precision=HIGHEST
        )
        both = nt(
            jnp.concatenate([fy_hi, fy_hi, fy_lo], axis=1),
            jnp.concatenate(
                [
                    jnp.concatenate([s_hi, s_lo, s_hi], axis=1),
                    jnp.concatenate([gx_hi, gx_lo, gx_hi], axis=1),
                ],
                axis=0,
            ),
        )
        n = s_hi.shape[0]
        gc_ref[rows, :] += both[:, :n]
        joint[j] += both[:, n:]
        gb_ref[rows, :] += nt(
            jnp.concatenate([gx_hi, gx_hi, gx_lo], axis=1),
            jnp.concatenate([e_hi, e_lo, e_hi], axis=1),
        )
        state = last * (mid * state + (tn(b, gx_hi) + tn(b, gx_lo)))

    @pl.when(group == pl.num_programs(0) - 1)
    def _():
        for j in range(chunks):
            rows = pl.ds(j * CHUNK, CHUNK)
            b, c = b_ref[rows, :], c_ref[rows, :]
            j_hi, j_lo = split(jnp.where(causal, joint[j], 0.0))
            gc_ref[rows, :] += nn(j_hi, b) + nn(j_lo, b)
            gb_ref[rows, :] += tn(j_hi, c) + tn(j_lo, c)


def on_device(peers, inputs, in_map, out_map, log_decay, cotangent):
    heads, tokens = log_decay.shape
    width = inputs.shape[1] // heads
    states = in_map.shape[1]
    groups = heads // GROUP
    columns = GROUP * width
    rates = log_decay.reshape(groups, GROUP, tokens)
    vmem = pl.BlockSpec(memory_space=pltpu.VMEM)
    channel_block = pl.BlockSpec((tokens, columns), lambda i: (0, i))
    map_block = pl.BlockSpec((tokens, states), lambda i: (0, 0))
    rate_block = pl.BlockSpec((1, GROUP, tokens), lambda i: (i, 0, 0))
    state_block = pl.BlockSpec((GROUP, states, width), lambda i: (i, 0, 0))
    state_shape = jax.ShapeDtypeStruct((heads, states, width), F32)
    params = pltpu.CompilerParams(
        dimension_semantics=("arbitrary",), vmem_limit_bytes=VMEM_BYTES
    )
    s_here, e_here, totals = pl.pallas_call(
        states_kernel,
        grid=(groups,),
        in_specs=[channel_block, map_block, map_block, rate_block, channel_block],
        out_specs=[state_block, state_block, pl.BlockSpec((GROUP, 8, width), lambda i: (i, 0, 0))],
        out_shape=[state_shape, state_shape, jax.ShapeDtypeStruct((heads, 8, width), F32)],
        compiler_params=params,
        name="shard_states",
    )(inputs, in_map, out_map, rates, cotangent)

    items = heads * SPLIT
    message = (items, states // SPLIT, width)
    message_shape = jax.ShapeDtypeStruct(message, F32)
    s_in, e_in = pl.pallas_call(
        functools.partial(chain_kernel, peers),
        in_specs=[vmem, vmem, vmem],
        out_specs=[vmem, vmem],
        out_shape=[message_shape, message_shape],
        scratch_shapes=[
            pltpu.VMEM(message, F32),
            pltpu.VMEM(message, F32),
            pltpu.SemaphoreType.DMA((items,)),
            pltpu.SemaphoreType.DMA((items,)),
            pltpu.SemaphoreType.DMA((items,)),
            pltpu.SemaphoreType.DMA((items,)),
        ],
        compiler_params=pltpu.CompilerParams(
            collective_id=0, has_side_effects=True, vmem_limit_bytes=VMEM_BYTES
        ),
        name="carry_chain",
    )(s_here.reshape(message), e_here.reshape(message), totals)
    s_in = s_in.reshape(heads, states, width)
    e_in = e_in.reshape(heads, states, width)

    map_shape = jax.ShapeDtypeStruct((tokens, states), F32)
    chunks = tokens // CHUNK
    grad_inputs, grad_in, grad_out, grad_rates = pl.pallas_call(
        grads_kernel,
        grid=(groups,),
        in_specs=[
            channel_block, map_block, map_block, rate_block, channel_block, state_block, state_block
        ],
        out_specs=[channel_block, map_block, map_block, rate_block],
        out_shape=[
            jax.ShapeDtypeStruct(inputs.shape, F32),
            map_shape,
            map_shape,
            jax.ShapeDtypeStruct(rates.shape, F32),
        ],
        scratch_shapes=[
            pltpu.VMEM((chunks + 1, states, columns), F32),
            pltpu.VMEM((tokens, columns), BF16),
            pltpu.VMEM((tokens, columns), BF16),
            pltpu.VMEM((chunks, CHUNK, CHUNK), F32),
        ],
        compiler_params=params,
        name="gradients",
    )(inputs, in_map, out_map, rates, cotangent, s_in, e_in)

    grad_in, grad_out = (
        lax.psum_scatter(g, "head", scatter_dimension=0, tiled=True) for g in (grad_in, grad_out)
    )
    return grad_inputs, grad_in, grad_out, grad_rates.reshape(heads, tokens)


def solution(mesh):
    placed = (P("seq", "head"), P("seq", None), P("seq", None), P("head", "seq"), P("seq", "head"))
    return jax.shard_map(
        functools.partial(on_device, mesh.shape["seq"]),
        mesh=mesh,
        in_specs=placed,
        out_specs=(
            P("seq", "head"),
            P(("seq", "head"), None),
            P(("seq", "head"), None),
            P("head", "seq"),
        ),
        check_vma=False,
    )
```

```python
import functools

import jax
import jax.numpy as jnp
from jax import lax
from jax.experimental import pallas as pl
from jax.experimental.pallas import tpu as pltpu
from jax.sharding import PartitionSpec as P

MESH = pl.DeviceIdType.MESH
F32, BF16 = jnp.float32, jnp.bfloat16
HIGHEST = lax.Precision.HIGHEST
CHUNK = 128
GROUP = 4
SPLIT = 2
SKEW = 2
VMEM_BYTES = 56 * 1024 * 1024


def nn(a, b, **kw):
    return lax.dot_general(a, b, (((1,), (0,)), ((), ())), preferred_element_type=F32, **kw)


def nt(a, b, **kw):
    return lax.dot_general(a, b, (((1,), (1,)), ((), ())), preferred_element_type=F32, **kw)


def tn(a, b, **kw):
    return lax.dot_general(a, b, (((0,), (0,)), ((), ())), preferred_element_type=F32, **kw)


def split(v):
    hi = v.astype(BF16)
    return hi, (v - hi.astype(F32)).astype(BF16)


def order():
    row = lax.broadcasted_iota(jnp.int32, (CHUNK, CHUNK), 0)
    col = lax.broadcasted_iota(jnp.int32, (CHUNK, CHUNK), 1)
    return row >= col


def wide(v, width):
    rows, heads = v.shape
    return jnp.concatenate(
        [jnp.broadcast_to(v[:, h : h + 1], (rows, width)) for h in range(heads)], axis=1
    )


def heads_of(v, width):
    return [v[:, h : h + width] for h in range(0, v.shape[1], width)]


def per_head(v, heads):
    rows = v.shape[0]
    lane = lax.broadcasted_iota(jnp.int32, (rows, heads), 1)
    out = jnp.zeros((rows, heads), F32)
    for h, part in enumerate(heads_of(v, v.shape[1] // heads)):
        out = jnp.where(lane == h, jnp.sum(part, axis=1, keepdims=True), out)
    return out


def running_of(rates):
    upper = jnp.logical_not(order()).astype(F32) + (
        lax.broadcasted_iota(jnp.int32, (CHUNK, CHUNK), 0)
        == lax.broadcasted_iota(jnp.int32, (CHUNK, CHUNK), 1)
    ).astype(F32)
    return nn(rates, upper, precision=HIGHEST)


def shard_decays(rates, heads):
    rows = rates.shape[0]
    run = running_of(rates)
    row = lax.broadcasted_iota(jnp.int32, (rows, rows), 0)
    col = lax.broadcasted_iota(jnp.int32, (rows, rows), 1)
    same = lax.rem(row, heads) == lax.rem(col, heads)
    last = run[:, CHUNK - 1 : CHUNK]
    wide_last = jnp.broadcast_to(last, run.shape)
    earlier = nn(jnp.logical_and(same, col < row).astype(F32), wide_last, precision=HIGHEST)
    later = nn(jnp.logical_and(same, col > row).astype(F32), wide_last, precision=HIGHEST)
    from_start = (jnp.exp(earlier) * jnp.exp(run)).T
    to_end = jnp.exp(later + (last - run)).T
    return from_start, to_end, from_start[CHUNK - 1 : CHUNK, rows - heads :]


def states_kernel(x_ref, b_ref, c_ref, rate_ref, dy_ref, s_ref, e_ref, total_ref):
    tokens, columns = x_ref.shape
    heads, width = s_ref.shape[0], s_ref.shape[2]
    from_start, to_end, total = shard_decays(rate_ref[0], heads)

    def scaled(ref, factors):
        parts = []
        for j in range(tokens // CHUNK):
            rows = pl.ds(j * CHUNK, CHUNK)
            cols = factors[:, j * heads : (j + 1) * heads]
            parts.append(split(wide(cols, width) * ref[rows, :].astype(F32)))
        return jnp.concatenate([hi for hi, _ in parts] + [lo for _, lo in parts], axis=0)

    def twice(ref):
        turned = ref[...].T
        return jnp.concatenate([turned, turned], axis=1)

    state = nn(twice(b_ref), scaled(x_ref, to_end))
    adjoint = nn(twice(c_ref), scaled(dy_ref, from_start))
    for h, (s, e) in enumerate(zip(heads_of(state, width), heads_of(adjoint, width))):
        s_ref[h] = s
        e_ref[h] = e
        total_ref[h] = jnp.broadcast_to(total[:, h : h + 1], total_ref.shape[1:])


def chain_kernel(
    peers, groups, s_ref, e_ref, total_ref, x_ref, b_ref, c_ref, rate_ref, dy_ref,
    s_in, e_in, gx_ref, gb_ref, gc_ref, rates_out,
    s_out, e_out, s_send, s_recv, e_send, e_recv,
    f_ref, g_ref, end_ref, scores_ref, adjoints, fy_hi_ref, fy_lo_ref, state_ref, joint,
):
    me, lane = lax.axis_index("seq"), lax.axis_index("head")
    items = s_ref.shape[0]
    has_left, has_right = me > 0, me < peers - 1
    barrier = pltpu.get_barrier_semaphore()

    @pl.when(has_left)
    def _():
        pl.semaphore_signal(barrier, inc=1, device_id=(me - 1, lane), device_id_type=MESH)

    @pl.when(has_right)
    def _():
        pl.semaphore_signal(barrier, inc=1, device_id=(me + 1, lane), device_id_type=MESH)

    pl.semaphore_wait(barrier, jnp.where(has_left, 1, 0) + jnp.where(has_right, 1, 0))

    def forward(i):
        return pltpu.make_async_remote_copy(
            src_ref=s_out.at[i], dst_ref=s_in.at[i], send_sem=s_send.at[i], recv_sem=s_recv.at[i],
            device_id=(me + 1, lane), device_id_type=MESH,
        )

    def backward(i):
        return pltpu.make_async_remote_copy(
            src_ref=e_out.at[i], dst_ref=e_in.at[i], send_sem=e_send.at[i], recv_sem=e_recv.at[i],
            device_id=(me - 1, lane), device_id_type=MESH,
        )

    def pass_on(i, copy, has_source, has_target, local, come, out):
        @pl.when(has_source)
        def _():
            copy(i).wait_recv()

        @pl.when(jnp.logical_not(has_source))
        def _():
            come[i] = jnp.zeros(come.shape[1:], F32)

        @pl.when(has_target)
        def _():
            out[i] = total_ref[i // SPLIT][0:1, :] * come[i] + local[i]
            copy(i).start()


    tokens = x_ref.shape[0]
    chunks = tokens // CHUNK
    width = s_ref.shape[2]
    heads = rate_ref.shape[1] // chunks
    columns = heads * width
    states = b_ref.shape[1]
    pairs = chunks // 2
    period = chunks + pairs
    causal = order()
    after = jnp.logical_not(causal).astype(F32)

    gb_ref[...] = jnp.zeros_like(gb_ref)
    gc_ref[...] = jnp.zeros_like(gc_ref)
    joint[...] = jnp.zeros_like(joint)

    def prepare(group):
        run = running_of(rate_ref[group])
        mid = run[:, CHUNK // 2 - 1 : CHUNK // 2]
        f = jnp.exp(run - mid)
        f_cols, g_cols = f.T, jnp.exp(mid - run).T
        m_cols = jnp.broadcast_to(jnp.exp(mid), run.shape).T
        for j in range(chunks):
            at = slice(j * heads, (j + 1) * heads)
            f_ref[j] = f_cols[:, at]
            g_ref[j] = g_cols[:, at]
            end_ref[j, 0:1, :] = wide(m_cols[0:1, at], width)
            end_ref[j, 1:2, :] = wide(f_cols[CHUNK - 1 : CHUNK, at], width)

    def scores_of(j, _):
        rows = pl.ds(pl.multiple_of(j * CHUNK, CHUNK), CHUNK)
        scores = jnp.where(causal, nt(c_ref[rows, :], b_ref[rows, :]), 0.0)
        for k, part in enumerate(split(scores) + split(scores.T)):
            scores_ref[j, k] = part
        return 0

    def backward_chunk(group, j):
        rows = pl.ds(pl.multiple_of(j * CHUNK, CHUNK), CHUNK)
        cols = pl.ds(pl.multiple_of(group * columns, columns), columns)
        mid, last = end_ref[j, 0:1, :], end_ref[j, 1:2, :]
        fy_hi, fy_lo = split(wide(f_ref[j], width) * dy_ref[rows, cols].astype(F32))
        fy_hi_ref[rows, :] = fy_hi
        fy_lo_ref[rows, :] = fy_lo
        c = c_ref[rows, :].T
        part = nn(jnp.concatenate([c, c], axis=1), jnp.concatenate([fy_hi, fy_lo], axis=0))
        adjoints[j] = mid * (last * adjoints[j + 1] + part)

    def forward_chunk(group, j):
        rows = pl.ds(pl.multiple_of(j * CHUNK, CHUNK), CHUNK)
        cols = pl.ds(pl.multiple_of(group * columns, columns), columns)
        mid, last = end_ref[j, 0:1, :], end_ref[j, 1:2, :]
        g_wide = wide(g_ref[j], width)
        b, c = b_ref[rows, :], c_ref[rows, :]
        gx = g_wide * x_ref[rows, cols].astype(F32)
        gx_hi, gx_lo = split(gx)
        fy_hi, fy_lo = fy_hi_ref[rows, :], fy_lo_ref[rows, :]
        m_hi, m_lo, t_hi, t_lo = (scores_ref[j, k] for k in range(4))
        state = state_ref[...]
        s_hi, s_lo = split(mid * state)
        e_hi, e_lo = split(last * adjoints[j + 1])
        y = nn(
            jnp.concatenate([m_hi, m_hi, m_lo, c, c], axis=1),
            jnp.concatenate([gx_hi, gx_lo, gx_hi, s_hi, s_lo], axis=0),
        )
        z = nn(
            jnp.concatenate([t_hi, t_hi, t_lo, b, b], axis=1),
            jnp.concatenate([fy_hi, fy_lo, fy_hi, e_hi, e_lo], axis=0),
        )
        gx_ref[rows, cols] = g_wide * z
        fy = fy_hi.astype(F32) + fy_lo.astype(F32)
        turnover = per_head(gx * z - fy * y, heads)
        crossing = per_head(adjoints[j] * state, heads)
        rates_out[group * chunks + j] = tn(turnover, after, precision=HIGHEST) + tn(
            crossing, jnp.ones((states, CHUNK), F32), precision=HIGHEST
        )
        both = nt(
            jnp.concatenate([fy_hi, fy_hi, fy_lo], axis=1),
            jnp.concatenate(
                [
                    jnp.concatenate([s_hi, s_lo, s_hi], axis=1),
                    jnp.concatenate([gx_hi, gx_lo, gx_hi], axis=1),
                ],
                axis=0,
            ),
        )
        gc_ref[rows, :] += both[:, :states]
        joint[j] += both[:, states:]
        gb_ref[rows, :] += nt(
            jnp.concatenate([gx_hi, gx_hi, gx_lo], axis=1),
            jnp.concatenate([e_hi, e_lo, e_hi], axis=1),
        )
        turned = b.T
        part = nn(jnp.concatenate([turned, turned], axis=1), jnp.concatenate([gx_hi, gx_lo], axis=0))
        state_ref[...] = last * (mid * state + part)

    def work(i):
        group, at = i // period, lax.rem(i, period)

        @pl.when(at == 0)
        def _():
            prepare(group)
            adjoints[chunks] = jnp.zeros((states, columns), F32)
            state_ref[...] = jnp.zeros_like(state_ref)

        @pl.when(at < pairs)
        def _():
            backward_chunk(group, chunks - 1 - 2 * at)
            backward_chunk(group, chunks - 2 - 2 * at)

        @pl.when(at >= pairs)
        def _():
            forward_chunk(group, at - pairs)

    def step(i, _):
        at_s, at_e = i - SKEW * me, i - SKEW * (peers - 1 - me)

        @pl.when(jnp.logical_and(at_s >= 0, at_s < items))
        def _():
            pass_on(at_s, forward, has_left, has_right, s_ref, s_in, s_out)

        @pl.when(jnp.logical_and(at_e >= 0, at_e < items))
        def _():
            pass_on(at_e, backward, has_right, has_left, e_ref, e_in, e_out)

        @pl.when(i == 0)
        def _():
            lax.fori_loop(0, chunks, scores_of, 0)

        @pl.when(i < groups * period)
        def _():
            work(i)

        return 0

    lax.fori_loop(0, max(items + SKEW * (peers - 1), groups * period), step, 0)

    def inner(j, _):
        rows = pl.ds(pl.multiple_of(j * CHUNK, CHUNK), CHUNK)
        b, c = b_ref[rows, :], c_ref[rows, :]
        j_hi, j_lo = split(jnp.where(causal, joint[j], 0.0))
        gc_ref[rows, :] += nn(j_hi, b) + nn(j_lo, b)
        gb_ref[rows, :] += tn(j_hi, c) + tn(j_lo, c)
        return 0

    lax.fori_loop(0, chunks, inner, 0)

    def finish(i, _):
        @pl.when(has_right)
        def _():
            forward(i).wait_send()

        @pl.when(has_left)
        def _():
            backward(i).wait_send()

        return 0

    lax.fori_loop(0, items, finish, 0)


def carried_kernel(
    x_ref, b_ref, c_ref, rate_ref, dy_ref, s_ref, e_ref, gx_here, gb_here, gc_here, rates_here,
    gx_ref, gb_ref, gc_ref, rates_out,
):
    tokens, columns = x_ref.shape
    heads, states, width = s_ref.shape
    chunks = tokens // CHUNK
    from_start, to_end, total = shard_decays(rate_ref[0], heads)
    causal = order()
    ordered = jnp.concatenate(
        [causal.astype(F32), jnp.logical_not(causal).astype(F32), jnp.ones((states, CHUNK), F32)],
        axis=0,
    )

    @pl.when(pl.program_id(0) == 0)
    def _():
        gb_ref[...] = gb_here[...]
        gc_ref[...] = gc_here[...]

    s_all = [s_ref[h] for h in range(heads)]
    e_all = [e_ref[h] for h in range(heads)]
    crossing = per_head(jnp.concatenate([s * e for s, e in zip(s_all, e_all)], axis=1), heads) * total
    s_parts = [jnp.concatenate(split(s), axis=1) for s in s_all]
    e_parts = [jnp.concatenate(split(e), axis=1) for e in e_all]
    e_rows = jnp.concatenate(split(jnp.concatenate(e_all, axis=1)), axis=0)
    lane = lax.broadcasted_iota(jnp.int32, (CHUNK, heads), 1)
    outs, ins = [], []
    for j in range(chunks):
        rows = pl.ds(j * CHUNK, CHUNK)
        at = slice(j * heads, (j + 1) * heads)
        fs, te = from_start[:, at], to_end[:, at]
        b, c = b_ref[rows, :], c_ref[rows, :]
        b_wide, c_wide = b.astype(F32), c.astype(F32)
        z = nn(jnp.concatenate([b, b], axis=1), e_rows)
        gb, gc = gb_ref[rows, :], gc_ref[rows, :]
        d_out = d_in = jnp.zeros((CHUNK, heads), F32)
        for h in range(heads):
            here = slice(h * width, (h + 1) * width)
            x, dy = x_ref[rows, here], dy_ref[rows, here]
            fs_h = jnp.broadcast_to(fs[:, h : h + 1], (CHUNK, width))
            te_h = jnp.broadcast_to(te[:, h : h + 1], (CHUNK, width))
            gx_ref[rows, here] = gx_here[rows, here] + te_h * z[:, here]
            feed_out = fs_h * nt(jnp.concatenate([dy, dy], axis=1), s_parts[h])
            feed_in = te_h * nt(jnp.concatenate([x, x], axis=1), e_parts[h])
            gc += feed_out
            gb += feed_in
            d_out = jnp.where(lane == h, jnp.sum(feed_out * c_wide, axis=1, keepdims=True), d_out)
            d_in = jnp.where(lane == h, jnp.sum(feed_in * b_wide, axis=1, keepdims=True), d_in)
        gb_ref[rows, :] = gb
        gc_ref[rows, :] = gc
        outs.append(d_out)
        ins.append(d_in)
    for j in range(chunks):
        beyond = crossing + sum(outs[j + 1 :]) + sum(ins[:j])
        terms = jnp.concatenate([outs[j], ins[j], beyond], axis=0)
        rates_out[0, :, pl.ds(j * CHUNK, CHUNK)] = rates_here[j] + tn(
            terms, ordered, precision=HIGHEST
        )


def scatter_kernel(peers, b_ref, c_ref, gb_ref, gc_ref, near, summed, far, sems):
    seq, me = lax.axis_index("seq"), lax.axis_index("head")
    rows = gb_ref.shape[0]
    rows_of = lambda q: pl.ds(pl.multiple_of(q * rows, rows), rows)
    chips = peers // 2
    core, chip = lax.rem(me, 2), me // 2
    other = me + 1 - 2 * core
    barrier = pltpu.get_barrier_semaphore()
    pl.semaphore_signal(barrier, inc=1, device_id=(seq, other), device_id_type=MESH)
    for k in range(1, chips):
        to = lax.rem(chip + k, chips) * 2 + core
        pl.semaphore_signal(barrier, inc=1, device_id=(seq, to), device_id_type=MESH)
    pl.semaphore_wait(barrier, chips)

    refs = (b_ref, c_ref)
    copies = []
    for k in list(range(1, chips)) + [0]:
        at = lax.rem(chip + k, chips)
        for m in range(2):
            copy = pltpu.make_async_remote_copy(
                src_ref=refs[m].at[rows_of(at * 2 + 1 - core)],
                dst_ref=near.at[k, m],
                send_sem=sems.at[0, k, m], recv_sem=sems.at[1, k, m],
                device_id=(seq, other), device_id_type=MESH,
            )
            copy.start()
            copies.append((k, m, at, copy))
    sent = []
    for k, m, at, copy in copies:
        copy.wait_recv()
        summed[k, m] = refs[m][rows_of(at * 2 + core), :] + near[k, m]
        if k:
            onward = pltpu.make_async_remote_copy(
                src_ref=summed.at[k, m], dst_ref=far.at[k, m],
                send_sem=sems.at[2, k, m], recv_sem=sems.at[3, k, m],
                device_id=(seq, at * 2 + core), device_id_type=MESH,
            )
            onward.start()
            sent.append((k, m, onward))
    totals = [summed[0, m] for m in range(2)]
    for k, m, onward in sent:
        onward.wait_recv()
        totals[m] = totals[m] + far[k, m]
    gb_ref[...] = totals[0]
    gc_ref[...] = totals[1]
    for _, _, _, copy in copies:
        copy.wait_send()
    for _, _, onward in sent:
        onward.wait_send()


def on_device(peers, head_peers, inputs, in_map, out_map, log_decay, cotangent):
    heads, tokens = log_decay.shape
    width = inputs.shape[1] // heads
    states = in_map.shape[1]
    groups = heads // GROUP
    columns = GROUP * width
    chunks = tokens // CHUNK
    rates = log_decay.reshape(groups, GROUP, chunks, CHUNK).transpose(0, 2, 1, 3)
    rates = rates.reshape(groups, chunks * GROUP, CHUNK)
    vmem = pl.BlockSpec(memory_space=pltpu.VMEM)
    channel_block = pl.BlockSpec((tokens, columns), lambda i: (0, i))
    map_block = pl.BlockSpec((tokens, states), lambda i: (0, 0))
    rate_block = pl.BlockSpec((1, chunks * GROUP, CHUNK), lambda i: (i, 0, 0))
    state_block = pl.BlockSpec((GROUP, states, width), lambda i: (i, 0, 0))
    state_shape = jax.ShapeDtypeStruct((heads, states, width), F32)
    channel_shape = jax.ShapeDtypeStruct(inputs.shape, F32)
    map_shape = jax.ShapeDtypeStruct((tokens, states), F32)
    params = pltpu.CompilerParams(
        dimension_semantics=("arbitrary",), vmem_limit_bytes=VMEM_BYTES
    )
    s_here, e_here, totals = pl.pallas_call(
        states_kernel,
        grid=(groups,),
        in_specs=[channel_block, map_block, map_block, rate_block, channel_block],
        out_specs=[state_block, state_block, pl.BlockSpec((GROUP, 8, width), lambda i: (i, 0, 0))],
        out_shape=[state_shape, state_shape, jax.ShapeDtypeStruct((heads, 8, width), F32)],
        compiler_params=params,
        name="shard_states",
    )(inputs, in_map, out_map, rates, cotangent)

    items = heads * SPLIT
    message = (items, states // SPLIT, width)
    message_shape = jax.ShapeDtypeStruct(message, F32)
    s_in, e_in, grad_inputs, grad_in, grad_out, grad_rates = pl.pallas_call(
        functools.partial(chain_kernel, peers, groups),
        in_specs=[vmem] * 8,
        out_specs=[vmem] * 6,
        out_shape=[
            message_shape, message_shape, channel_shape, map_shape, map_shape,
            jax.ShapeDtypeStruct((groups * chunks, GROUP, CHUNK), F32),
        ],
        scratch_shapes=[
            pltpu.VMEM(message, F32),
            pltpu.VMEM(message, F32),
            pltpu.SemaphoreType.DMA((items,)),
            pltpu.SemaphoreType.DMA((items,)),
            pltpu.SemaphoreType.DMA((items,)),
            pltpu.SemaphoreType.DMA((items,)),
            pltpu.VMEM((chunks, CHUNK, GROUP), F32),
            pltpu.VMEM((chunks, CHUNK, GROUP), F32),
            pltpu.VMEM((chunks, 8, columns), F32),
            pltpu.VMEM((chunks, 4, CHUNK, CHUNK), BF16),
            pltpu.VMEM((chunks + 1, states, columns), F32),
            pltpu.VMEM((tokens, columns), BF16),
            pltpu.VMEM((tokens, columns), BF16),
            pltpu.VMEM((states, columns), F32),
            pltpu.VMEM((chunks, CHUNK, CHUNK), F32),
        ],
        compiler_params=pltpu.CompilerParams(
            collective_id=0, has_side_effects=True, vmem_limit_bytes=VMEM_BYTES
        ),
        name="carry_chain",
    )(
        s_here.reshape(message), e_here.reshape(message), totals,
        inputs, in_map, out_map, rates, cotangent,
    )
    s_in = s_in.reshape(heads, states, width)
    e_in = e_in.reshape(heads, states, width)

    grad_inputs, grad_in, grad_out, grad_rates = pl.pallas_call(
        carried_kernel,
        grid=(groups,),
        in_specs=[
            channel_block, map_block, map_block, rate_block, channel_block, state_block, state_block,
            channel_block, map_block, map_block,
            pl.BlockSpec((chunks, GROUP, CHUNK), lambda i: (i, 0, 0)),
        ],
        out_specs=[
            channel_block, map_block, map_block,
            pl.BlockSpec((1, GROUP, tokens), lambda i: (i, 0, 0)),
        ],
        out_shape=[
            channel_shape, map_shape, map_shape, jax.ShapeDtypeStruct((groups, GROUP, tokens), F32)
        ],
        compiler_params=params,
        name="carried_gradients",
    )(
        inputs, in_map, out_map, rates, cotangent, s_in, e_in,
        grad_inputs, grad_in, grad_out, grad_rates,
    )

    rows = tokens // head_peers
    chips = head_peers // 2
    piece = jax.ShapeDtypeStruct((rows, states), F32)
    grad_in, grad_out = pl.pallas_call(
        functools.partial(scatter_kernel, head_peers),
        in_specs=[vmem, vmem],
        out_specs=[vmem, vmem],
        out_shape=[piece, piece],
        scratch_shapes=[
            pltpu.VMEM((chips, 2, rows, states), F32),
            pltpu.VMEM((chips, 2, rows, states), F32),
            pltpu.VMEM((chips, 2, rows, states), F32),
            pltpu.SemaphoreType.DMA((4, chips, 2)),
        ],
        compiler_params=pltpu.CompilerParams(
            collective_id=1, has_side_effects=True, vmem_limit_bytes=VMEM_BYTES
        ),
        name="map_scatter",
    )(grad_in, grad_out)
    return grad_inputs, grad_in, grad_out, grad_rates.reshape(heads, tokens)


def solution(mesh):
    placed = (P("seq", "head"), P("seq", None), P("seq", None), P("head", "seq"), P("seq", "head"))
    return jax.shard_map(
        functools.partial(on_device, mesh.shape["seq"], mesh.shape["head"]),
        mesh=mesh,
        in_specs=placed,
        out_specs=(
            P("seq", "head"),
            P(("seq", "head"), None),
            P(("seq", "head"), None),
            P("head", "seq"),
        ),
        check_vma=False,
    )
```

```python
import functools

import jax
import jax.numpy as jnp
from jax import lax
from jax.experimental import pallas as pl
from jax.experimental.pallas import tpu as pltpu
from jax.sharding import PartitionSpec as P

MESH = pl.DeviceIdType.MESH
F32, BF16 = jnp.float32, jnp.bfloat16
HIGHEST = lax.Precision.HIGHEST
CHUNK = 128
GROUP = 4
SPLIT = 2
SKEW = 2
VMEM_BYTES = 56 * 1024 * 1024


def nn(a, b, **kw):
    return lax.dot_general(a, b, (((1,), (0,)), ((), ())), preferred_element_type=F32, **kw)


def nt(a, b, **kw):
    return lax.dot_general(a, b, (((1,), (1,)), ((), ())), preferred_element_type=F32, **kw)


def tn(a, b, **kw):
    return lax.dot_general(a, b, (((0,), (0,)), ((), ())), preferred_element_type=F32, **kw)


def split(v):
    hi = v.astype(BF16)
    return hi, (v - hi.astype(F32)).astype(BF16)


def order():
    row = lax.broadcasted_iota(jnp.int32, (CHUNK, CHUNK), 0)
    col = lax.broadcasted_iota(jnp.int32, (CHUNK, CHUNK), 1)
    return row >= col


def wide(v, width):
    rows, heads = v.shape
    return jnp.concatenate(
        [jnp.broadcast_to(v[:, h : h + 1], (rows, width)) for h in range(heads)], axis=1
    )


def heads_of(v, width):
    return [v[:, h : h + width] for h in range(0, v.shape[1], width)]


def per_head(v, heads):
    rows = v.shape[0]
    lane = lax.broadcasted_iota(jnp.int32, (rows, heads), 1)
    out = jnp.zeros((rows, heads), F32)
    for h, part in enumerate(heads_of(v, v.shape[1] // heads)):
        out = jnp.where(lane == h, jnp.sum(part, axis=1, keepdims=True), out)
    return out


def running_of(rates):
    upper = jnp.logical_not(order()).astype(F32) + (
        lax.broadcasted_iota(jnp.int32, (CHUNK, CHUNK), 0)
        == lax.broadcasted_iota(jnp.int32, (CHUNK, CHUNK), 1)
    ).astype(F32)
    return nn(rates, upper, precision=HIGHEST)


def shard_decays(rates, heads):
    rows = rates.shape[0]
    run = running_of(rates)
    row = lax.broadcasted_iota(jnp.int32, (rows, rows), 0)
    col = lax.broadcasted_iota(jnp.int32, (rows, rows), 1)
    same = lax.rem(row, heads) == lax.rem(col, heads)
    last = run[:, CHUNK - 1 : CHUNK]
    wide_last = jnp.broadcast_to(last, run.shape)
    earlier = nn(jnp.logical_and(same, col < row).astype(F32), wide_last, precision=HIGHEST)
    later = nn(jnp.logical_and(same, col > row).astype(F32), wide_last, precision=HIGHEST)
    from_start = (jnp.exp(earlier) * jnp.exp(run)).T
    to_end = jnp.exp(later + (last - run)).T
    return from_start, to_end, from_start[CHUNK - 1 : CHUNK, rows - heads :]


def states_kernel(x_ref, b_ref, c_ref, rate_ref, dy_ref, s_ref, e_ref, total_ref):
    tokens, columns = x_ref.shape
    heads, width = s_ref.shape[0], s_ref.shape[2]
    from_start, to_end, total = shard_decays(rate_ref[0], heads)

    def scaled(ref, factors):
        parts = []
        for j in range(tokens // CHUNK):
            rows = pl.ds(j * CHUNK, CHUNK)
            cols = factors[:, j * heads : (j + 1) * heads]
            parts.append(split(wide(cols, width) * ref[rows, :].astype(F32)))
        return jnp.concatenate([hi for hi, _ in parts] + [lo for _, lo in parts], axis=0)

    def twice(ref):
        turned = ref[...].T
        return jnp.concatenate([turned, turned], axis=1)

    state = nn(twice(b_ref), scaled(x_ref, to_end))
    adjoint = nn(twice(c_ref), scaled(dy_ref, from_start))
    for h, (s, e) in enumerate(zip(heads_of(state, width), heads_of(adjoint, width))):
        s_ref[h] = s
        e_ref[h] = e
        total_ref[h] = jnp.broadcast_to(total[:, h : h + 1], total_ref.shape[1:])


def chain_kernel(
    peers, groups, s_ref, e_ref, total_ref, x_ref, b_ref, c_ref, rate_ref, dy_ref,
    s_in, e_in, gx_ref, gb_ref, gc_ref, rates_out,
    s_out, e_out, s_send, s_recv, e_send, e_recv,
    f_ref, g_ref, end_ref, scores_ref, adjoints, fy_hi_ref, fy_lo_ref, state_ref, joint,
):
    me, lane = lax.axis_index("seq"), lax.axis_index("head")
    items = s_ref.shape[0]
    has_left, has_right = me > 0, me < peers - 1
    barrier = pltpu.get_barrier_semaphore()

    @pl.when(has_left)
    def _():
        pl.semaphore_signal(barrier, inc=1, device_id=(me - 1, lane), device_id_type=MESH)

    @pl.when(has_right)
    def _():
        pl.semaphore_signal(barrier, inc=1, device_id=(me + 1, lane), device_id_type=MESH)

    pl.semaphore_wait(barrier, jnp.where(has_left, 1, 0) + jnp.where(has_right, 1, 0))

    def forward(i):
        return pltpu.make_async_remote_copy(
            src_ref=s_out.at[i], dst_ref=s_in.at[i], send_sem=s_send.at[i], recv_sem=s_recv.at[i],
            device_id=(me + 1, lane), device_id_type=MESH,
        )

    def backward(i):
        return pltpu.make_async_remote_copy(
            src_ref=e_out.at[i], dst_ref=e_in.at[i], send_sem=e_send.at[i], recv_sem=e_recv.at[i],
            device_id=(me - 1, lane), device_id_type=MESH,
        )

    def pass_on(i, copy, has_source, has_target, local, come, out):
        @pl.when(has_source)
        def _():
            copy(i).wait_recv()

        @pl.when(jnp.logical_not(has_source))
        def _():
            come[i] = jnp.zeros(come.shape[1:], F32)

        @pl.when(has_target)
        def _():
            out[i] = total_ref[i // SPLIT][0:1, :] * come[i] + local[i]
            copy(i).start()


    tokens = x_ref.shape[0]
    chunks = tokens // CHUNK
    width = s_ref.shape[2]
    heads = rate_ref.shape[1] // chunks
    columns = heads * width
    states = b_ref.shape[1]
    pairs = chunks // 2
    period = chunks + pairs
    causal = order()

    gb_ref[...] = jnp.zeros_like(gb_ref)
    gc_ref[...] = jnp.zeros_like(gc_ref)
    joint[...] = jnp.zeros_like(joint)

    def prepare(group):
        run = running_of(rate_ref[group])
        mid = run[:, CHUNK // 2 - 1 : CHUNK // 2]
        f = jnp.exp(run - mid)
        f_cols, g_cols = f.T, jnp.exp(mid - run).T
        m_cols = jnp.broadcast_to(jnp.exp(mid), run.shape).T
        for j in range(chunks):
            at = slice(j * heads, (j + 1) * heads)
            f_ref[j] = f_cols[:, at]
            g_ref[j] = g_cols[:, at]
            end_ref[j, 0:1, :] = wide(m_cols[0:1, at], width)
            end_ref[j, 1:2, :] = wide(f_cols[CHUNK - 1 : CHUNK, at], width)

    def scores_of(j, _):
        rows = pl.ds(pl.multiple_of(j * CHUNK, CHUNK), CHUNK)
        scores = jnp.where(causal, nt(c_ref[rows, :], b_ref[rows, :]), 0.0)
        for k, part in enumerate(split(scores) + split(scores.T)):
            scores_ref[j, k] = part
        return 0

    def backward_chunk(group, j):
        rows = pl.ds(pl.multiple_of(j * CHUNK, CHUNK), CHUNK)
        cols = pl.ds(pl.multiple_of(group * columns, columns), columns)
        mid, last = end_ref[j, 0:1, :], end_ref[j, 1:2, :]
        fy_hi, fy_lo = split(wide(f_ref[j], width) * dy_ref[rows, cols].astype(F32))
        fy_hi_ref[rows, :] = fy_hi
        fy_lo_ref[rows, :] = fy_lo
        c = c_ref[rows, :].T
        part = nn(jnp.concatenate([c, c], axis=1), jnp.concatenate([fy_hi, fy_lo], axis=0))
        adjoints[j] = mid * (last * adjoints[j + 1] + part)

    def forward_chunk(group, j):
        rows = pl.ds(pl.multiple_of(j * CHUNK, CHUNK), CHUNK)
        cols = pl.ds(pl.multiple_of(group * columns, columns), columns)
        mid, last = end_ref[j, 0:1, :], end_ref[j, 1:2, :]
        g_wide = wide(g_ref[j], width)
        b, c = b_ref[rows, :], c_ref[rows, :]
        gx = g_wide * x_ref[rows, cols].astype(F32)
        gx_hi, gx_lo = split(gx)
        fy_hi, fy_lo = fy_hi_ref[rows, :], fy_lo_ref[rows, :]
        m_hi, m_lo, t_hi, t_lo = (scores_ref[j, k] for k in range(4))
        state = state_ref[...]
        s_hi, s_lo = split(mid * state)
        e_hi, e_lo = split(last * adjoints[j + 1])
        y = nn(
            jnp.concatenate([m_hi, m_hi, m_lo, c, c], axis=1),
            jnp.concatenate([gx_hi, gx_lo, gx_hi, s_hi, s_lo], axis=0),
        )
        z = nn(
            jnp.concatenate([t_hi, t_hi, t_lo, b, b], axis=1),
            jnp.concatenate([fy_hi, fy_lo, fy_hi, e_hi, e_lo], axis=0),
        )
        gx_ref[rows, cols] = g_wide * z
        fy = fy_hi.astype(F32) + fy_lo.astype(F32)
        turnover = jnp.concatenate([gx * z - fy * y, adjoints[j] * state], axis=1)
        rates_out[group * chunks + j] = per_head(turnover, 2 * heads)
        both = nt(
            jnp.concatenate([fy_hi, fy_hi, fy_lo], axis=1),
            jnp.concatenate(
                [
                    jnp.concatenate([s_hi, s_lo, s_hi], axis=1),
                    jnp.concatenate([gx_hi, gx_lo, gx_hi], axis=1),
                ],
                axis=0,
            ),
        )
        gc_ref[rows, :] += both[:, :states]
        joint[j] += both[:, states:]
        gb_ref[rows, :] += nt(
            jnp.concatenate([gx_hi, gx_hi, gx_lo], axis=1),
            jnp.concatenate([e_hi, e_lo, e_hi], axis=1),
        )
        turned = b.T
        part = nn(jnp.concatenate([turned, turned], axis=1), jnp.concatenate([gx_hi, gx_lo], axis=0))
        state_ref[...] = last * (mid * state + part)

    def work(i):
        group, at = i // period, lax.rem(i, period)

        @pl.when(at == 0)
        def _():
            prepare(group)
            adjoints[chunks] = jnp.zeros((states, columns), F32)
            state_ref[...] = jnp.zeros_like(state_ref)

        @pl.when(at < pairs)
        def _():
            backward_chunk(group, chunks - 1 - 2 * at)
            backward_chunk(group, chunks - 2 - 2 * at)

        @pl.when(at >= pairs)
        def _():
            forward_chunk(group, at - pairs)

    def step(i, _):
        at_s, at_e = i - SKEW * me, i - SKEW * (peers - 1 - me)

        @pl.when(jnp.logical_and(at_s >= 0, at_s < items))
        def _():
            pass_on(at_s, forward, has_left, has_right, s_ref, s_in, s_out)

        @pl.when(jnp.logical_and(at_e >= 0, at_e < items))
        def _():
            pass_on(at_e, backward, has_right, has_left, e_ref, e_in, e_out)

        @pl.when(i == 0)
        def _():
            lax.fori_loop(0, chunks, scores_of, 0)

        @pl.when(i < groups * period)
        def _():
            work(i)

        return 0

    lax.fori_loop(0, max(items + SKEW * (peers - 1), groups * period), step, 0)

    def inner(j, _):
        rows = pl.ds(pl.multiple_of(j * CHUNK, CHUNK), CHUNK)
        b, c = b_ref[rows, :], c_ref[rows, :]
        j_hi, j_lo = split(jnp.where(causal, joint[j], 0.0))
        gc_ref[rows, :] += nn(j_hi, b) + nn(j_lo, b)
        gb_ref[rows, :] += tn(j_hi, c) + tn(j_lo, c)
        return 0

    lax.fori_loop(0, chunks, inner, 0)

    def finish(i, _):
        @pl.when(has_right)
        def _():
            forward(i).wait_send()

        @pl.when(has_left)
        def _():
            backward(i).wait_send()

        return 0

    lax.fori_loop(0, items, finish, 0)


def carried_kernel(
    x_ref, b_ref, c_ref, rate_ref, dy_ref, s_ref, e_ref, gx_here, gb_here, gc_here, rates_here,
    gx_ref, gb_ref, gc_ref, rates_out,
):
    tokens, columns = x_ref.shape
    heads, states, width = s_ref.shape
    chunks = tokens // CHUNK
    from_start, to_end, total = shard_decays(rate_ref[0], heads)
    causal = order()
    ordered = jnp.concatenate(
        [causal.astype(F32), jnp.logical_not(causal).astype(F32), jnp.ones((states, CHUNK), F32)],
        axis=0,
    )

    @pl.when(pl.program_id(0) == 0)
    def _():
        gb_ref[...] = gb_here[...]
        gc_ref[...] = gc_here[...]

    s_all = [s_ref[h] for h in range(heads)]
    e_all = [e_ref[h] for h in range(heads)]
    crossing = per_head(jnp.concatenate([s * e for s, e in zip(s_all, e_all)], axis=1), heads) * total
    lane = lax.broadcasted_iota(jnp.int32, (CHUNK, heads), 1)
    outs = [jnp.zeros((CHUNK, heads), F32)] * chunks
    ins = [rates_here[j][:, :heads] for j in range(chunks)]
    b, c = b_ref[...], c_ref[...]
    b_twice = jnp.concatenate([b, b], axis=1)
    for h in range(heads):
        here = slice(h * width, (h + 1) * width)
        x, dy = x_ref[:, here], dy_ref[:, here]
        e_parts = split(e_all[h])
        z = nn(b_twice, jnp.concatenate(e_parts, axis=0))
        feed_out = nt(
            jnp.concatenate([dy, dy], axis=1), jnp.concatenate(split(s_all[h]), axis=1)
        )
        feed_in = nt(jnp.concatenate([x, x], axis=1), jnp.concatenate(e_parts, axis=1))
        for j in range(chunks):
            rows = slice(j * CHUNK, (j + 1) * CHUNK)
            col = j * heads + h
            fs = jnp.broadcast_to(from_start[:, col : col + 1], (CHUNK, width))
            te = jnp.broadcast_to(to_end[:, col : col + 1], (CHUNK, width))
            gx_ref[rows, here] = gx_here[rows, here] + te * z[rows, :]
            out, back = fs * feed_out[rows, :], te * feed_in[rows, :]
            gc_ref[rows, :] += out
            gb_ref[rows, :] += back
            out_sum = jnp.sum(out * c[rows, :].astype(F32), axis=1, keepdims=True)
            in_sum = jnp.sum(back * b[rows, :].astype(F32), axis=1, keepdims=True)
            outs[j] = jnp.where(lane == h, out_sum, outs[j])
            ins[j] = jnp.where(lane == h, ins[j] + in_sum, ins[j])
    beyond = []
    for j in range(chunks):
        others = crossing + rates_here[j][:, heads:]
        for k in range(chunks):
            if k > j:
                others = others + outs[k]
            elif k < j:
                others = others + (ins[k] - rates_here[k][:, :heads])
        beyond.append(others)
    terms = jnp.concatenate(
        [jnp.concatenate(part, axis=1) for part in (outs, ins, beyond)], axis=0
    )
    sums = tn(terms, ordered, precision=HIGHEST)
    for k in range(rates_out.shape[0] // heads):

        @pl.when(pl.program_id(0) == k)
        def _():
            for j in range(chunks):
                rates_out[pl.ds(k * heads, heads), pl.ds(j * CHUNK, CHUNK)] = sums[
                    j * heads : (j + 1) * heads, :
                ]


def scatter_kernel(peers, b_ref, c_ref, gb_ref, gc_ref, near, summed, far, sems):
    seq, me = lax.axis_index("seq"), lax.axis_index("head")
    rows = gb_ref.shape[0]
    rows_of = lambda q: pl.ds(pl.multiple_of(q * rows, rows), rows)
    chips = peers // 2
    core, chip = lax.rem(me, 2), me // 2
    other = me + 1 - 2 * core
    barrier = pltpu.get_barrier_semaphore()
    pl.semaphore_signal(barrier, inc=1, device_id=(seq, other), device_id_type=MESH)
    for k in range(1, chips):
        to = lax.rem(chip + k, chips) * 2 + core
        pl.semaphore_signal(barrier, inc=1, device_id=(seq, to), device_id_type=MESH)
    pl.semaphore_wait(barrier, chips)

    refs = (b_ref, c_ref)
    copies = []
    for k in list(range(1, chips)) + [0]:
        at = lax.rem(chip + k, chips)
        for m in range(2):
            copy = pltpu.make_async_remote_copy(
                src_ref=refs[m].at[rows_of(at * 2 + 1 - core)],
                dst_ref=near.at[k, m],
                send_sem=sems.at[0, k, m], recv_sem=sems.at[1, k, m],
                device_id=(seq, other), device_id_type=MESH,
            )
            copy.start()
            copies.append((k, m, at, copy))
    sent = []
    for k, m, at, copy in copies:
        copy.wait_recv()
        summed[k, m] = refs[m][rows_of(at * 2 + core), :] + near[k, m]
        if k:
            onward = pltpu.make_async_remote_copy(
                src_ref=summed.at[k, m], dst_ref=far.at[k, m],
                send_sem=sems.at[2, k, m], recv_sem=sems.at[3, k, m],
                device_id=(seq, at * 2 + core), device_id_type=MESH,
            )
            onward.start()
            sent.append((k, m, onward))
    totals = [summed[0, m] for m in range(2)]
    for k, m, onward in sent:
        onward.wait_recv()
        totals[m] = totals[m] + far[k, m]
    gb_ref[...] = totals[0]
    gc_ref[...] = totals[1]
    for _, _, _, copy in copies:
        copy.wait_send()
    for _, _, onward in sent:
        onward.wait_send()


def on_device(peers, head_peers, inputs, in_map, out_map, log_decay, cotangent):
    heads, tokens = log_decay.shape
    width = inputs.shape[1] // heads
    states = in_map.shape[1]
    groups = heads // GROUP
    columns = GROUP * width
    chunks = tokens // CHUNK
    rates = log_decay.reshape(groups, GROUP, chunks, CHUNK).transpose(0, 2, 1, 3)
    rates = rates.reshape(groups, chunks * GROUP, CHUNK)
    vmem = pl.BlockSpec(memory_space=pltpu.VMEM)
    channel_block = pl.BlockSpec((tokens, columns), lambda i: (0, i))
    map_block = pl.BlockSpec((tokens, states), lambda i: (0, 0))
    rate_block = pl.BlockSpec((1, chunks * GROUP, CHUNK), lambda i: (i, 0, 0))
    state_block = pl.BlockSpec((GROUP, states, width), lambda i: (i, 0, 0))
    state_shape = jax.ShapeDtypeStruct((heads, states, width), F32)
    channel_shape = jax.ShapeDtypeStruct(inputs.shape, F32)
    map_shape = jax.ShapeDtypeStruct((tokens, states), F32)
    params = pltpu.CompilerParams(
        dimension_semantics=("arbitrary",), vmem_limit_bytes=VMEM_BYTES
    )
    s_here, e_here, totals = pl.pallas_call(
        states_kernel,
        grid=(groups,),
        in_specs=[channel_block, map_block, map_block, rate_block, channel_block],
        out_specs=[state_block, state_block, pl.BlockSpec((GROUP, 8, width), lambda i: (i, 0, 0))],
        out_shape=[state_shape, state_shape, jax.ShapeDtypeStruct((heads, 8, width), F32)],
        compiler_params=params,
        name="shard_states",
    )(inputs, in_map, out_map, rates, cotangent)

    items = heads * SPLIT
    message = (items, states // SPLIT, width)
    message_shape = jax.ShapeDtypeStruct(message, F32)
    s_in, e_in, grad_inputs, grad_in, grad_out, grad_rates = pl.pallas_call(
        functools.partial(chain_kernel, peers, groups),
        in_specs=[vmem] * 8,
        out_specs=[vmem] * 6,
        out_shape=[
            message_shape, message_shape, channel_shape, map_shape, map_shape,
            jax.ShapeDtypeStruct((groups * chunks, CHUNK, 2 * GROUP), F32),
        ],
        scratch_shapes=[
            pltpu.VMEM(message, F32),
            pltpu.VMEM(message, F32),
            pltpu.SemaphoreType.DMA((items,)),
            pltpu.SemaphoreType.DMA((items,)),
            pltpu.SemaphoreType.DMA((items,)),
            pltpu.SemaphoreType.DMA((items,)),
            pltpu.VMEM((chunks, CHUNK, GROUP), F32),
            pltpu.VMEM((chunks, CHUNK, GROUP), F32),
            pltpu.VMEM((chunks, 8, columns), F32),
            pltpu.VMEM((chunks, 4, CHUNK, CHUNK), BF16),
            pltpu.VMEM((chunks + 1, states, columns), F32),
            pltpu.VMEM((tokens, columns), BF16),
            pltpu.VMEM((tokens, columns), BF16),
            pltpu.VMEM((states, columns), F32),
            pltpu.VMEM((chunks, CHUNK, CHUNK), F32),
        ],
        compiler_params=pltpu.CompilerParams(
            collective_id=0, has_side_effects=True, vmem_limit_bytes=VMEM_BYTES
        ),
        name="carry_chain",
    )(
        s_here.reshape(message), e_here.reshape(message), totals,
        inputs, in_map, out_map, rates, cotangent,
    )
    s_in = s_in.reshape(heads, states, width)
    e_in = e_in.reshape(heads, states, width)

    grad_inputs, grad_in, grad_out, grad_rates = pl.pallas_call(
        carried_kernel,
        grid=(groups,),
        in_specs=[
            channel_block, map_block, map_block, rate_block, channel_block, state_block, state_block,
            channel_block, map_block, map_block,
            pl.BlockSpec((chunks, CHUNK, 2 * GROUP), lambda i: (i, 0, 0)),
        ],
        out_specs=[
            channel_block, map_block, map_block,
            pl.BlockSpec((heads, tokens), lambda i: (0, 0)),
        ],
        out_shape=[
            channel_shape, map_shape, map_shape, jax.ShapeDtypeStruct((heads, tokens), F32)
        ],
        compiler_params=params,
        name="carried_gradients",
    )(
        inputs, in_map, out_map, rates, cotangent, s_in, e_in,
        grad_inputs, grad_in, grad_out, grad_rates,
    )

    rows = tokens // head_peers
    chips = head_peers // 2
    piece = jax.ShapeDtypeStruct((rows, states), F32)
    grad_in, grad_out = pl.pallas_call(
        functools.partial(scatter_kernel, head_peers),
        in_specs=[vmem, vmem],
        out_specs=[vmem, vmem],
        out_shape=[piece, piece],
        scratch_shapes=[
            pltpu.VMEM((chips, 2, rows, states), F32),
            pltpu.VMEM((chips, 2, rows, states), F32),
            pltpu.VMEM((chips, 2, rows, states), F32),
            pltpu.SemaphoreType.DMA((4, chips, 2)),
        ],
        compiler_params=pltpu.CompilerParams(
            collective_id=1, has_side_effects=True, vmem_limit_bytes=VMEM_BYTES
        ),
        name="map_scatter",
    )(grad_in, grad_out)
    return grad_inputs, grad_in, grad_out, grad_rates


def solution(mesh):
    placed = (P("seq", "head"), P("seq", None), P("seq", None), P("head", "seq"), P("seq", "head"))
    return jax.shard_map(
        functools.partial(on_device, mesh.shape["seq"], mesh.shape["head"]),
        mesh=mesh,
        in_specs=placed,
        out_specs=(
            P("seq", "head"),
            P(("seq", "head"), None),
            P(("seq", "head"), None),
            P("head", "seq"),
        ),
        check_vma=False,
    )
```

```python
import functools

import jax
import jax.numpy as jnp
from jax import lax
from jax.experimental import pallas as pl
from jax.experimental.pallas import tpu as pltpu
from jax.sharding import PartitionSpec as P

MESH = pl.DeviceIdType.MESH
F32, BF16 = jnp.float32, jnp.bfloat16
HIGHEST = lax.Precision.HIGHEST
CHUNK = 128
GROUP = 4
SPLIT = 2
SKEW = 2
VMEM_BYTES = 56 * 1024 * 1024


def nn(a, b, **kw):
    return lax.dot_general(a, b, (((1,), (0,)), ((), ())), preferred_element_type=F32, **kw)


def nt(a, b, **kw):
    return lax.dot_general(a, b, (((1,), (1,)), ((), ())), preferred_element_type=F32, **kw)


def tn(a, b, **kw):
    return lax.dot_general(a, b, (((0,), (0,)), ((), ())), preferred_element_type=F32, **kw)


def split(v):
    hi = v.astype(BF16)
    return hi, (v - hi.astype(F32)).astype(BF16)


def order():
    row = lax.broadcasted_iota(jnp.int32, (CHUNK, CHUNK), 0)
    col = lax.broadcasted_iota(jnp.int32, (CHUNK, CHUNK), 1)
    return row >= col


def wide(v, width):
    rows, heads = v.shape
    return jnp.concatenate(
        [jnp.broadcast_to(v[:, h : h + 1], (rows, width)) for h in range(heads)], axis=1
    )


def heads_of(v, width):
    return [v[:, h : h + width] for h in range(0, v.shape[1], width)]


def per_head(v, heads):
    rows = v.shape[0]
    lane = lax.broadcasted_iota(jnp.int32, (rows, heads), 1)
    out = jnp.zeros((rows, heads), F32)
    for h, part in enumerate(heads_of(v, v.shape[1] // heads)):
        out = jnp.where(lane == h, jnp.sum(part, axis=1, keepdims=True), out)
    return out


def columns_of(v):
    hi = v.astype(BF16).astype(F32)
    mid = (v - hi).astype(BF16).astype(F32)
    return jnp.concatenate([hi, mid, v - hi - mid], axis=0).T.astype(BF16)


def fill_spread(spread_ref, heads, width):
    chunks, depth, columns = spread_ref.shape
    row = lax.rem(lax.broadcasted_iota(jnp.int32, (depth, columns), 0), depth // 3)
    head = lax.div(lax.broadcasted_iota(jnp.int32, (depth, columns), 1), width)
    for j in range(chunks):
        spread_ref[j] = (row == head + j * heads).astype(F32).astype(BF16)


def fill_gather(gather_ref, width):
    shape = gather_ref.shape
    row = lax.div(lax.broadcasted_iota(jnp.int32, shape, 0), width)
    gather_ref[...] = (row == lax.broadcasted_iota(jnp.int32, shape, 1)).astype(F32).astype(BF16)


def head_sums(v, gather_ref):
    hi, lo = split(v)
    sums = gather_ref[...]
    return nn(hi, sums) + nn(lo, sums)


def running_of(rates):
    upper = jnp.logical_not(order()).astype(F32) + (
        lax.broadcasted_iota(jnp.int32, (CHUNK, CHUNK), 0)
        == lax.broadcasted_iota(jnp.int32, (CHUNK, CHUNK), 1)
    ).astype(F32)
    return nn(rates, upper, precision=HIGHEST)


def shard_decays(rates, heads):
    rows = rates.shape[0]
    run = running_of(rates)
    row = lax.broadcasted_iota(jnp.int32, (rows, rows), 0)
    col = lax.broadcasted_iota(jnp.int32, (rows, rows), 1)
    same = lax.rem(row, heads) == lax.rem(col, heads)
    last = run[:, CHUNK - 1 : CHUNK]
    wide_last = jnp.broadcast_to(last, run.shape)
    earlier = nn(jnp.logical_and(same, col < row).astype(F32), wide_last, precision=HIGHEST)
    later = nn(jnp.logical_and(same, col > row).astype(F32), wide_last, precision=HIGHEST)
    from_start = jnp.exp(earlier) * jnp.exp(run)
    to_end = jnp.exp(later + (last - run))
    total = from_start.T[CHUNK - 1 : CHUNK, rows - heads :]
    return columns_of(from_start), columns_of(to_end), total


def states_kernel(x_ref, b_ref, c_ref, rate_ref, dy_ref, s_ref, e_ref, total_ref, spread_ref):
    tokens, columns = x_ref.shape
    heads, width = s_ref.shape[0], s_ref.shape[2]

    @pl.when(pl.program_id(0) == 0)
    def _():
        fill_spread(spread_ref, heads, width)

    from_start, to_end, total = shard_decays(rate_ref[0], heads)

    def scaled(ref, factors):
        parts = []
        for j in range(tokens // CHUNK):
            rows = pl.ds(j * CHUNK, CHUNK)
            parts.append(split(nn(factors, spread_ref[j]) * ref[rows, :].astype(F32)))
        return jnp.concatenate([hi for hi, _ in parts] + [lo for _, lo in parts], axis=0)

    def twice(ref):
        turned = ref[...].T
        return jnp.concatenate([turned, turned], axis=1)

    state = nn(twice(b_ref), scaled(x_ref, to_end))
    adjoint = nn(twice(c_ref), scaled(dy_ref, from_start))
    for h, (s, e) in enumerate(zip(heads_of(state, width), heads_of(adjoint, width))):
        s_ref[h] = s
        e_ref[h] = e
        total_ref[h] = jnp.broadcast_to(total[:, h : h + 1], total_ref.shape[1:])


def chain_kernel(
    peers, groups, s_ref, e_ref, total_ref, x_ref, b_ref, c_ref, rate_ref, dy_ref,
    s_in, e_in, gx_ref, gb_ref, gc_ref, rates_out,
    s_out, e_out, s_send, s_recv, e_send, e_recv,
    f_ref, g_ref, end_ref, spread_ref, gather_ref, scores_ref, adjoints, fy_hi_ref, fy_lo_ref, state_ref, joint,
):
    me, lane = lax.axis_index("seq"), lax.axis_index("head")
    items = s_ref.shape[0]
    has_left, has_right = me > 0, me < peers - 1
    barrier = pltpu.get_barrier_semaphore()

    @pl.when(has_left)
    def _():
        pl.semaphore_signal(barrier, inc=1, device_id=(me - 1, lane), device_id_type=MESH)

    @pl.when(has_right)
    def _():
        pl.semaphore_signal(barrier, inc=1, device_id=(me + 1, lane), device_id_type=MESH)

    pl.semaphore_wait(barrier, jnp.where(has_left, 1, 0) + jnp.where(has_right, 1, 0))

    def forward(i):
        return pltpu.make_async_remote_copy(
            src_ref=s_out.at[i], dst_ref=s_in.at[i], send_sem=s_send.at[i], recv_sem=s_recv.at[i],
            device_id=(me + 1, lane), device_id_type=MESH,
        )

    def backward(i):
        return pltpu.make_async_remote_copy(
            src_ref=e_out.at[i], dst_ref=e_in.at[i], send_sem=e_send.at[i], recv_sem=e_recv.at[i],
            device_id=(me - 1, lane), device_id_type=MESH,
        )

    def pass_on(i, copy, has_source, has_target, local, come, out):
        @pl.when(has_source)
        def _():
            copy(i).wait_recv()

        @pl.when(jnp.logical_not(has_source))
        def _():
            come[i] = jnp.zeros(come.shape[1:], F32)

        @pl.when(has_target)
        def _():
            out[i] = total_ref[i // SPLIT][0:1, :] * come[i] + local[i]
            copy(i).start()


    tokens = x_ref.shape[0]
    chunks = tokens // CHUNK
    width = s_ref.shape[2]
    heads = rate_ref.shape[1] // chunks
    columns = heads * width
    states = b_ref.shape[1]
    pairs = chunks // 2
    period = chunks + pairs
    causal = order()

    fill_spread(spread_ref, heads, width)
    fill_gather(gather_ref, width)
    gb_ref[...] = jnp.zeros_like(gb_ref)
    gc_ref[...] = jnp.zeros_like(gc_ref)
    joint[...] = jnp.zeros_like(joint)

    def prepare(group):
        run = running_of(rate_ref[group])
        mid = run[:, CHUNK // 2 - 1 : CHUNK // 2]
        f = jnp.exp(run - mid)
        f_cols = f.T
        f_ref[...] = columns_of(f)
        g_ref[...] = columns_of(jnp.exp(mid - run))
        m_cols = jnp.broadcast_to(jnp.exp(mid), run.shape).T
        for j in range(chunks):
            at = slice(j * heads, (j + 1) * heads)
            end_ref[j, 0:1, :] = wide(m_cols[0:1, at], width)
            end_ref[j, 1:2, :] = wide(f_cols[CHUNK - 1 : CHUNK, at], width)

    def scores_of(j, _):
        rows = pl.ds(pl.multiple_of(j * CHUNK, CHUNK), CHUNK)
        scores = jnp.where(causal, nt(c_ref[rows, :], b_ref[rows, :]), 0.0)
        for k, part in enumerate(split(scores) + split(scores.T)):
            scores_ref[j, k] = part
        return 0

    def backward_chunk(group, j):
        rows = pl.ds(pl.multiple_of(j * CHUNK, CHUNK), CHUNK)
        cols = pl.ds(pl.multiple_of(group * columns, columns), columns)
        mid, last = end_ref[j, 0:1, :], end_ref[j, 1:2, :]
        fy_hi, fy_lo = split(nn(f_ref[...], spread_ref[j]) * dy_ref[rows, cols].astype(F32))
        fy_hi_ref[rows, :] = fy_hi
        fy_lo_ref[rows, :] = fy_lo
        c = c_ref[rows, :].T
        part = nn(jnp.concatenate([c, c], axis=1), jnp.concatenate([fy_hi, fy_lo], axis=0))
        adjoints[j] = mid * (last * adjoints[j + 1] + part)

    def forward_chunk(group, j):
        rows = pl.ds(pl.multiple_of(j * CHUNK, CHUNK), CHUNK)
        cols = pl.ds(pl.multiple_of(group * columns, columns), columns)
        mid, last = end_ref[j, 0:1, :], end_ref[j, 1:2, :]
        g_wide = nn(g_ref[...], spread_ref[j])
        b, c = b_ref[rows, :], c_ref[rows, :]
        gx = g_wide * x_ref[rows, cols].astype(F32)
        gx_hi, gx_lo = split(gx)
        fy_hi, fy_lo = fy_hi_ref[rows, :], fy_lo_ref[rows, :]
        m_hi, m_lo, t_hi, t_lo = (scores_ref[j, k] for k in range(4))
        state = state_ref[...]
        s_hi, s_lo = split(mid * state)
        e_hi, e_lo = split(last * adjoints[j + 1])
        y = nn(
            jnp.concatenate([m_hi, m_hi, m_lo, c, c], axis=1),
            jnp.concatenate([gx_hi, gx_lo, gx_hi, s_hi, s_lo], axis=0),
        )
        z = nn(
            jnp.concatenate([t_hi, t_hi, t_lo, b, b], axis=1),
            jnp.concatenate([fy_hi, fy_lo, fy_hi, e_hi, e_lo], axis=0),
        )
        gx_ref[rows, cols] = g_wide * z
        fy = fy_hi.astype(F32) + fy_lo.astype(F32)
        turnover = jnp.concatenate([gx * z - fy * y, adjoints[j] * state], axis=1)
        rates_out[group * chunks + j] = head_sums(turnover, gather_ref)
        both = nt(
            jnp.concatenate([fy_hi, fy_hi, fy_lo], axis=1),
            jnp.concatenate(
                [
                    jnp.concatenate([s_hi, s_lo, s_hi], axis=1),
                    jnp.concatenate([gx_hi, gx_lo, gx_hi], axis=1),
                ],
                axis=0,
            ),
        )
        gc_ref[rows, :] += both[:, :states]
        joint[j] += both[:, states:]
        gb_ref[rows, :] += nt(
            jnp.concatenate([gx_hi, gx_hi, gx_lo], axis=1),
            jnp.concatenate([e_hi, e_lo, e_hi], axis=1),
        )
        turned = b.T
        part = nn(jnp.concatenate([turned, turned], axis=1), jnp.concatenate([gx_hi, gx_lo], axis=0))
        state_ref[...] = last * (mid * state + part)

    def work(i):
        group, at = i // period, lax.rem(i, period)

        @pl.when(at == 0)
        def _():
            prepare(group)
            adjoints[chunks] = jnp.zeros((states, columns), F32)
            state_ref[...] = jnp.zeros_like(state_ref)

        @pl.when(at < pairs)
        def _():
            backward_chunk(group, chunks - 1 - 2 * at)
            backward_chunk(group, chunks - 2 - 2 * at)

        @pl.when(at >= pairs)
        def _():
            forward_chunk(group, at - pairs)

    def step(i, _):
        at_s, at_e = i - SKEW * me, i - SKEW * (peers - 1 - me)

        @pl.when(jnp.logical_and(at_s >= 0, at_s < items))
        def _():
            pass_on(at_s, forward, has_left, has_right, s_ref, s_in, s_out)

        @pl.when(jnp.logical_and(at_e >= 0, at_e < items))
        def _():
            pass_on(at_e, backward, has_right, has_left, e_ref, e_in, e_out)

        @pl.when(i == 0)
        def _():
            lax.fori_loop(0, chunks, scores_of, 0)

        @pl.when(i < groups * period)
        def _():
            work(i)

        return 0

    lax.fori_loop(0, max(items + SKEW * (peers - 1), groups * period), step, 0)

    def inner(j, _):
        rows = pl.ds(pl.multiple_of(j * CHUNK, CHUNK), CHUNK)
        b, c = b_ref[rows, :], c_ref[rows, :]
        j_hi, j_lo = split(jnp.where(causal, joint[j], 0.0))
        gc_ref[rows, :] += nn(j_hi, b) + nn(j_lo, b)
        gb_ref[rows, :] += tn(j_hi, c) + tn(j_lo, c)
        return 0

    lax.fori_loop(0, chunks, inner, 0)

    def finish(i, _):
        @pl.when(has_right)
        def _():
            forward(i).wait_send()

        @pl.when(has_left)
        def _():
            backward(i).wait_send()

        return 0

    lax.fori_loop(0, items, finish, 0)


def carried_kernel(
    x_ref, b_ref, c_ref, rate_ref, dy_ref, s_ref, e_ref, gx_here, gb_here, gc_here, rates_here,
    gx_ref, gb_ref, gc_ref, rates_out, spread_ref, gather_ref,
):
    tokens, columns = x_ref.shape
    heads, states, width = s_ref.shape
    chunks = tokens // CHUNK
    from_start, to_end, total = shard_decays(rate_ref[0], heads)
    causal = order()
    ordered = jnp.concatenate(
        [causal.astype(F32), jnp.logical_not(causal).astype(F32), jnp.ones((states, CHUNK), F32)],
        axis=0,
    )

    @pl.when(pl.program_id(0) == 0)
    def _():
        fill_spread(spread_ref, heads, width)
        fill_gather(gather_ref, width)
        gb_ref[...] = gb_here[...]
        gc_ref[...] = gc_here[...]

    s_all = [s_ref[h] for h in range(heads)]
    e_all = [e_ref[h] for h in range(heads)]
    crossing = per_head(jnp.concatenate([s * e for s, e in zip(s_all, e_all)], axis=1), heads) * total
    s_parts = [jnp.concatenate(split(s), axis=1) for s in s_all]
    e_parts = [jnp.concatenate(split(e), axis=1) for e in e_all]
    e_rows = jnp.concatenate(split(jnp.concatenate(e_all, axis=1)), axis=0)

    def feed(ref, rows, parts):
        out = []
        for h in range(heads):
            v = ref[rows, pl.ds(h * width, width)]
            out.append(nt(jnp.concatenate([v, v], axis=1), parts[h]))
        return jnp.concatenate(out, axis=1)

    outs, carried, ins = [], [], []
    for j in range(chunks):
        rows = pl.ds(j * CHUNK, CHUNK)
        b, c = b_ref[rows, :], c_ref[rows, :]
        fs, te = nn(from_start, spread_ref[j]), nn(to_end, spread_ref[j])
        gx_ref[rows, :] = gx_here[rows, :] + te * nn(jnp.concatenate([b, b], axis=1), e_rows)
        out, back = fs * feed(dy_ref, rows, s_parts), te * feed(x_ref, rows, e_parts)
        gc_ref[rows, :] += sum(heads_of(out, width))
        gb_ref[rows, :] += sum(heads_of(back, width))
        b_wide = jnp.concatenate([b.astype(F32)] * heads, axis=1)
        c_wide = jnp.concatenate([c.astype(F32)] * heads, axis=1)
        both = head_sums(jnp.concatenate([out * c_wide, back * b_wide], axis=1), gather_ref)
        outs.append(both[:, :heads])
        carried.append(both[:, heads:])
        ins.append(both[:, heads:] + rates_here[j][:, :heads])
    beyond = []
    for j in range(chunks):
        others = crossing + rates_here[j][:, heads:]
        for k in range(chunks):
            if k > j:
                others = others + outs[k]
            elif k < j:
                others = others + carried[k]
        beyond.append(others)
    terms = jnp.concatenate(
        [jnp.concatenate(part, axis=1) for part in (outs, ins, beyond)], axis=0
    )
    sums = tn(terms, ordered, precision=HIGHEST)
    for k in range(rates_out.shape[0] // heads):

        @pl.when(pl.program_id(0) == k)
        def _():
            for j in range(chunks):
                rates_out[pl.ds(k * heads, heads), pl.ds(j * CHUNK, CHUNK)] = sums[
                    j * heads : (j + 1) * heads, :
                ]


def scatter_kernel(peers, b_ref, c_ref, gb_ref, gc_ref, near, summed, far, sems):
    seq, me = lax.axis_index("seq"), lax.axis_index("head")
    rows = gb_ref.shape[0]
    rows_of = lambda q: pl.ds(pl.multiple_of(q * rows, rows), rows)
    chips = peers // 2
    core, chip = lax.rem(me, 2), me // 2
    other = me + 1 - 2 * core
    barrier = pltpu.get_barrier_semaphore()
    pl.semaphore_signal(barrier, inc=1, device_id=(seq, other), device_id_type=MESH)
    for k in range(1, chips):
        to = lax.rem(chip + k, chips) * 2 + core
        pl.semaphore_signal(barrier, inc=1, device_id=(seq, to), device_id_type=MESH)
    pl.semaphore_wait(barrier, chips)

    refs = (b_ref, c_ref)
    copies = []
    for k in list(range(1, chips)) + [0]:
        at = lax.rem(chip + k, chips)
        for m in range(2):
            copy = pltpu.make_async_remote_copy(
                src_ref=refs[m].at[rows_of(at * 2 + 1 - core)],
                dst_ref=near.at[k, m],
                send_sem=sems.at[0, k, m], recv_sem=sems.at[1, k, m],
                device_id=(seq, other), device_id_type=MESH,
            )
            copy.start()
            copies.append((k, m, at, copy))
    sent = []
    for k, m, at, copy in copies:
        copy.wait_recv()
        summed[k, m] = refs[m][rows_of(at * 2 + core), :] + near[k, m]
        if k:
            onward = pltpu.make_async_remote_copy(
                src_ref=summed.at[k, m], dst_ref=far.at[k, m],
                send_sem=sems.at[2, k, m], recv_sem=sems.at[3, k, m],
                device_id=(seq, at * 2 + core), device_id_type=MESH,
            )
            onward.start()
            sent.append((k, m, onward))
    totals = [summed[0, m] for m in range(2)]
    for k, m, onward in sent:
        onward.wait_recv()
        totals[m] = totals[m] + far[k, m]
    gb_ref[...] = totals[0]
    gc_ref[...] = totals[1]
    for _, _, _, copy in copies:
        copy.wait_send()
    for _, _, onward in sent:
        onward.wait_send()


def on_device(peers, head_peers, inputs, in_map, out_map, log_decay, cotangent):
    heads, tokens = log_decay.shape
    width = inputs.shape[1] // heads
    states = in_map.shape[1]
    groups = heads // GROUP
    columns = GROUP * width
    chunks = tokens // CHUNK
    rates = log_decay.reshape(groups, GROUP, chunks, CHUNK).transpose(0, 2, 1, 3)
    rates = rates.reshape(groups, chunks * GROUP, CHUNK)
    vmem = pl.BlockSpec(memory_space=pltpu.VMEM)
    channel_block = pl.BlockSpec((tokens, columns), lambda i: (0, i))
    map_block = pl.BlockSpec((tokens, states), lambda i: (0, 0))
    rate_block = pl.BlockSpec((1, chunks * GROUP, CHUNK), lambda i: (i, 0, 0))
    state_block = pl.BlockSpec((GROUP, states, width), lambda i: (i, 0, 0))
    state_shape = jax.ShapeDtypeStruct((heads, states, width), F32)
    channel_shape = jax.ShapeDtypeStruct(inputs.shape, F32)
    map_shape = jax.ShapeDtypeStruct((tokens, states), F32)
    params = pltpu.CompilerParams(
        dimension_semantics=("arbitrary",), vmem_limit_bytes=VMEM_BYTES
    )
    spread = pltpu.VMEM((chunks, 3 * chunks * GROUP, columns), BF16)
    gather = pltpu.VMEM((2 * columns, 2 * GROUP), BF16)
    s_here, e_here, totals = pl.pallas_call(
        states_kernel,
        grid=(groups,),
        in_specs=[channel_block, map_block, map_block, rate_block, channel_block],
        out_specs=[state_block, state_block, pl.BlockSpec((GROUP, 8, width), lambda i: (i, 0, 0))],
        out_shape=[state_shape, state_shape, jax.ShapeDtypeStruct((heads, 8, width), F32)],
        scratch_shapes=[spread],
        compiler_params=params,
        name="shard_states",
    )(inputs, in_map, out_map, rates, cotangent)

    items = heads * SPLIT
    message = (items, states // SPLIT, width)
    message_shape = jax.ShapeDtypeStruct(message, F32)
    s_in, e_in, grad_inputs, grad_in, grad_out, grad_rates = pl.pallas_call(
        functools.partial(chain_kernel, peers, groups),
        in_specs=[vmem] * 8,
        out_specs=[vmem] * 6,
        out_shape=[
            message_shape, message_shape, channel_shape, map_shape, map_shape,
            jax.ShapeDtypeStruct((groups * chunks, CHUNK, 2 * GROUP), F32),
        ],
        scratch_shapes=[
            pltpu.VMEM(message, F32),
            pltpu.VMEM(message, F32),
            pltpu.SemaphoreType.DMA((items,)),
            pltpu.SemaphoreType.DMA((items,)),
            pltpu.SemaphoreType.DMA((items,)),
            pltpu.SemaphoreType.DMA((items,)),
            pltpu.VMEM((CHUNK, 3 * chunks * GROUP), BF16),
            pltpu.VMEM((CHUNK, 3 * chunks * GROUP), BF16),
            pltpu.VMEM((chunks, 8, columns), F32),
            spread,
            gather,
            pltpu.VMEM((chunks, 4, CHUNK, CHUNK), BF16),
            pltpu.VMEM((chunks + 1, states, columns), F32),
            pltpu.VMEM((tokens, columns), BF16),
            pltpu.VMEM((tokens, columns), BF16),
            pltpu.VMEM((states, columns), F32),
            pltpu.VMEM((chunks, CHUNK, CHUNK), F32),
        ],
        compiler_params=pltpu.CompilerParams(
            collective_id=0, has_side_effects=True, vmem_limit_bytes=VMEM_BYTES
        ),
        name="carry_chain",
    )(
        s_here.reshape(message), e_here.reshape(message), totals,
        inputs, in_map, out_map, rates, cotangent,
    )
    s_in = s_in.reshape(heads, states, width)
    e_in = e_in.reshape(heads, states, width)

    grad_inputs, grad_in, grad_out, grad_rates = pl.pallas_call(
        carried_kernel,
        grid=(groups,),
        in_specs=[
            channel_block, map_block, map_block, rate_block, channel_block, state_block, state_block,
            channel_block, map_block, map_block,
            pl.BlockSpec((chunks, CHUNK, 2 * GROUP), lambda i: (i, 0, 0)),
        ],
        out_specs=[
            channel_block, map_block, map_block,
            pl.BlockSpec((heads, tokens), lambda i: (0, 0)),
        ],
        out_shape=[
            channel_shape, map_shape, map_shape, jax.ShapeDtypeStruct((heads, tokens), F32)
        ],
        scratch_shapes=[spread, gather],
        compiler_params=params,
        name="carried_gradients",
    )(
        inputs, in_map, out_map, rates, cotangent, s_in, e_in,
        grad_inputs, grad_in, grad_out, grad_rates,
    )

    rows = tokens // head_peers
    chips = head_peers // 2
    piece = jax.ShapeDtypeStruct((rows, states), F32)
    grad_in, grad_out = pl.pallas_call(
        functools.partial(scatter_kernel, head_peers),
        in_specs=[vmem, vmem],
        out_specs=[vmem, vmem],
        out_shape=[piece, piece],
        scratch_shapes=[
            pltpu.VMEM((chips, 2, rows, states), F32),
            pltpu.VMEM((chips, 2, rows, states), F32),
            pltpu.VMEM((chips, 2, rows, states), F32),
            pltpu.SemaphoreType.DMA((4, chips, 2)),
        ],
        compiler_params=pltpu.CompilerParams(
            collective_id=1, has_side_effects=True, vmem_limit_bytes=VMEM_BYTES
        ),
        name="map_scatter",
    )(grad_in, grad_out)
    return grad_inputs, grad_in, grad_out, grad_rates


def solution(mesh):
    placed = (P("seq", "head"), P("seq", None), P("seq", None), P("head", "seq"), P("seq", "head"))
    return jax.shard_map(
        functools.partial(on_device, mesh.shape["seq"], mesh.shape["head"]),
        mesh=mesh,
        in_specs=placed,
        out_specs=(
            P("seq", "head"),
            P(("seq", "head"), None),
            P(("seq", "head"), None),
            P("head", "seq"),
        ),
        check_vma=False,
    )
```
